32 devices in a mesh: dp: 2 (over core), row: 4 (over y, x), col: 4 (over z).
Axes of the slice: x: 2, y: 2, z: 4, core: 2. Of those that a mesh axis runs over, the one named last changes fastest.
Arguments:
- forget_tokens: bfloat16 [256, 6144], P('dp', 'col'), may hold values from -6 to 6
- forget_cotangent: bfloat16 [256, 6144], P('dp', 'col'), may hold values from -6 to 6
- forget_labels: int32 [256], P('dp'), may hold values 0 or 1
- retain_tokens: bfloat16 [256, 6144], P('dp', 'col'), may hold values from -6 to 6
- ln_gain: float32 [6144], P('col'), may hold values from 0.25 to 1.75
- w_in: bfloat16 [6144, 24576], P('col', 'row'), may hold values from -0.078125 to 0.078125
- b_in: float32 [24576], P('row'), may hold values from -3 to 3
- w_out: bfloat16 [24576, 6144], P('row', 'col'), may hold values from -0.0390625 to 0.0390625
- b_out: float32 [6144], P('col'), may hold values from -3 to 3
- pruned: int32 [512], P('row'), may hold values from 0 to 24575, as said below
Outputs:
- saliency: float32 [24576], P('row')
- retain_out: bfloat16 [256, 6144], P(('dp', 'row'), 'col')
The draws below stay inside these ranges and needn't reach their ends.
Inputs may be any that keep to these rules, and one draw needn't show every extreme that they name: `pruned`: entries r * 128 to (r + 1) * 128 - 1 are distinct neurons that all lie in the r-th of the equal neuron ranges of the row shards.
All inputs are finite; a program needn't handle non-finite values. No bound on the sum of `forget_labels` on one device may be relied on, other than what follows from the above.
Results may differ from the reference program's by a relative error of at most 0.0052.
Values may be sent and summed in bfloat16 or wider, within the bound.
A program may use at most 256 MiB of HBM per device.

```python
import jax
import jax.numpy as jnp
from jax import lax

D = 6144
FF = 24576
PR_DEV = 128
NF = 256
NR = 256
N_ROW = 4


def draw_pruned(key, part):
    width = FF // N_ROW

    def one_shard(shard):
        order = jax.random.permutation(jax.random.fold_in(key, shard), width)
        return order[:PR_DEV].astype(jnp.int32) + shard * width
    shards = jnp.arange(N_ROW, dtype=jnp.int32)
    return jax.vmap(one_shard)(shards).reshape(-1).astype(jnp.int32)


def set_ends(values, key, smallest, top_value):
    spot = [jax.random.randint(jax.random.fold_in(key, axis), (), 0, length) for axis, length in enumerate(values.shape)]
    longest = values.shape.index(max(values.shape))
    neighbour = spot[:longest] + [(spot[longest] + 1) % values.shape[longest]] + spot[longest + 1:]
    return values.at[tuple(spot)].set(smallest).at[tuple(neighbour)].set(top_value)


def level_of(own_key, shape, cuts, smallest, top_value):
    def one(dim, parts):
        steps = jax.random.uniform(jax.random.fold_in(jax.random.fold_in(own_key, 6), dim), (parts,), jnp.float32, smallest / len(cuts), top_value / len(cuts))
        return jnp.repeat(jnp.exp(steps), shape[dim] // parts).reshape((-1,) + (1,) * (len(shape) - dim - 1))

    loudness = one(*cuts[0])
    for cut in cuts[1:]:
        loudness = loudness * one(*cut)
    return loudness


def noise(own_key, dims, scale, most, cuts=(), kind=jnp.bfloat16):
    values = scale * jax.random.normal(own_key, dims, jnp.float32)
    if cuts:
        values = values * level_of(own_key, dims, cuts, -0.22, 0.18)
    return jnp.clip(values, -most, most).astype(kind)


def setup_inputs(seed: int = 0) -> dict:
    seeds = jax.random.split(jax.random.key(seed), 11)
    return {
        "forget_tokens": noise(seeds[0], (NF, D), 1.0, 6.0, ((0, 2), (1, 4))),
        "forget_cotangent": noise(seeds[1], (NF, D), 1.0, 6.0, ((0, 2), (1, 4))),
        "forget_labels": set_ends((jax.random.randint(seeds[2], (NF,), 0, 2) < 1).astype(jnp.int32), jax.random.fold_in(seeds[2], 1), 0, 1),
        "retain_tokens": noise(seeds[3], (NR, D), 1.0, 6.0, ((0, 2), (1, 4))),
        "ln_gain": jnp.clip(1.0 + 0.15 * jax.random.normal(seeds[4], (D,), jnp.float32), 0.25, 1.75),
        "w_in": noise(seeds[5], (D, FF), D ** -0.5, 0.078125, ((0, 4), (1, 4))),
        "b_in": noise(seeds[6], (FF,), 0.5, 3.0, ((0, 4),), jnp.float32),
        "w_out": noise(seeds[7], (FF, D), FF ** -0.5, 0.0390625, ((0, 4), (1, 4))),
        "b_out": noise(seeds[8], (D,), 0.5, 3.0, ((0, 4),), jnp.float32),
        "pruned": draw_pruned(jax.random.fold_in(seeds[10], 71), 0),
    }


def layer_norm(x, gain):
    xf = x.astype(jnp.float32)
    mean_val = lax.optimization_barrier(jnp.mean(xf, axis=1, keepdims=True))
    centred = xf - mean_val
    var_val = lax.optimization_barrier(jnp.mean(centred * centred, axis=1, keepdims=True))
    return (centred * lax.rsqrt(var_val + 1e-06) * gain).astype(jnp.bfloat16)

def gelu_exact(v):
    return v * 0.5 * (1.0 + lax.erf(v * 0.7071067811865476))

def gelu_slope(v):
    return 0.5 * (1.0 + lax.erf(v * 0.7071067811865476)) + v * jnp.exp(-0.5 * v * v) * 0.3989422804014327

def reference(forget_tokens, forget_cotangent, forget_labels, retain_tokens, ln_gain, w_in, b_in, w_out, b_out, pruned):
    normed_f = layer_norm(forget_tokens, ln_gain)
    normed_r = layer_norm(retain_tokens, ln_gain)
    pre_f = jnp.dot(normed_f, w_in, preferred_element_type=jnp.float32) + b_in
    pre_r = jnp.dot(normed_r, w_in, preferred_element_type=jnp.float32) + b_in
    act_f = gelu_exact(pre_f).astype(jnp.bfloat16)
    act_r = gelu_exact(pre_r).astype(jnp.bfloat16)
    grad_y = forget_cotangent * forget_labels[:, None].astype(jnp.bfloat16)
    grad_w_out = jnp.dot(act_f.T, grad_y, preferred_element_type=jnp.float32)
    grad_act = jnp.dot(grad_y, w_out.T, preferred_element_type=jnp.float32)
    grad_pre = (grad_act * gelu_slope(pre_f)).astype(jnp.bfloat16)
    grad_w_in = jnp.dot(normed_f.T, grad_pre, preferred_element_type=jnp.float32)
    term_in = lax.optimization_barrier(jnp.sum(jnp.abs(w_in.astype(jnp.float32) * grad_w_in), axis=0))
    term_out = lax.optimization_barrier(jnp.sum(jnp.abs(w_out.astype(jnp.float32) * grad_w_out), axis=1))
    saliency = (term_in + term_out) / D
    keep = jnp.ones((FF,), jnp.float32).at[pruned].set(0.0).astype(jnp.bfloat16)
    masked_r = act_r * keep[None, :]
    retain_out = (jnp.dot(masked_r, w_out, preferred_element_type=jnp.float32) + b_out).astype(jnp.bfloat16)
    return (saliency, retain_out)
```

```python
import functools

import jax
import jax.numpy as jnp
from jax import lax
from jax.experimental import pallas as pl
from jax.experimental.pallas import tpu as pltpu
from jax.sharding import PartitionSpec as P

F32, BF16 = jnp.float32, jnp.bfloat16
MESH = pl.DeviceIdType.MESH
CHUNK = 256
LAG = 2


def dot(left, right, contract=((1,), (0,))):
    return lax.dot_general(left, right, (contract, ((), ())), preferred_element_type=F32)


def kernel(
    sizes,
    ft_hbm, rt_hbm, gy_hbm, win_hbm, wout_hbm, gain_ref, bin_ref, keep_ref, bout_ref,
    sal_out, ret_out,
    raw, gy, nrm, nrm_t, stats, win, wout, part, from_left, from_right, to_right, to_left,
    acc, half, blocks, mine, sal, sal_all, sal_fin,
    raw_loc, raw_send, raw_recv, st_send, st_recv, win_sem, wout_sem,
    right_send, right_recv, left_send, left_recv,
    half_send, half_recv, blk_send, blk_recv, sal_send, sal_recv, fin_send, fin_recv,
):
    cols, rows, tokens, nch = sizes
    width = nrm.shape[1]
    both = 2 * tokens
    dp, row, z = lax.axis_index("dp"), lax.axis_index("row"), lax.axis_index("col")
    other = 1 - dp

    def at_dp(d):
        return (d, row, z)

    def at_row(r):
        return (dp, r, z)

    def at_col(c):
        return (dp, row, c)

    def win_copy(c):
        lanes = pl.ds(pl.multiple_of((dp * nch + c) * CHUNK, CHUNK), CHUNK)
        return pltpu.make_async_copy(win_hbm.at[:, lanes], win.at[c], win_sem.at[c])

    def wout_copy(c):
        lines = pl.ds(pl.multiple_of((dp * nch + c) * CHUNK, CHUNK), CHUNK)
        return pltpu.make_async_copy(wout_hbm.at[lines, :], wout.at[c], wout_sem.at[c])

    sources = (ft_hbm, rt_hbm, gy_hbm)
    places = (raw.at[0, dp], raw.at[1, dp], gy.at[dp])
    own = [
        pltpu.make_async_copy(src, dst, raw_loc.at[i])
        for i, (src, dst) in enumerate(zip(sources, places))
    ]
    for copy in own:
        copy.start()

    @pl.loop(0, nch)
    def _(c):
        win_copy(c).start()
        wout_copy(c).start()

    barrier = pltpu.get_barrier_semaphore()
    pl.semaphore_signal(barrier, inc=1, device_id=at_dp(other), device_id_type=MESH)
    for o in range(1, cols):
        pl.semaphore_signal(
            barrier, inc=1, device_id=at_col(lax.rem(z + o, cols)), device_id_type=MESH
        )
    for o in range(1, rows):
        pl.semaphore_signal(
            barrier, inc=1, device_id=at_row(lax.rem(row + o, rows)), device_id_type=MESH
        )
    pl.semaphore_wait(barrier, 1 + (cols - 1) + (rows - 1))

    swaps = [
        pltpu.make_async_remote_copy(
            src_ref=src, dst_ref=dst, send_sem=raw_send.at[i], recv_sem=raw_recv.at[i],
            device_id=at_dp(other), device_id_type=MESH,
        )
        for i, (src, dst) in enumerate(zip(sources, places))
    ]
    for copy in swaps:
        copy.start()
    for copy in own:
        copy.wait()
    for copy in swaps:
        copy.wait()

    for kind in range(2):
        x = raw[kind].reshape(both, width).astype(F32)
        mean_here = jnp.sum(x, axis=1, keepdims=True) * (1.0 / width)
        cent = x - mean_here
        square = jnp.sum(cent * cent, axis=1, keepdims=True)
        lane = lax.broadcasted_iota(jnp.int32, (both, 128), 1)
        tile = jnp.where(lane == 0, mean_here, square)
        stats[z, :, kind * both : (kind + 1) * both] = jnp.transpose(tile)[0:8, :]
    stat_copies = [
        pltpu.make_async_remote_copy(
            src_ref=stats.at[z], dst_ref=stats.at[z],
            send_sem=st_send.at[o - 1], recv_sem=st_recv.at[o - 1],
            device_id=at_col(lax.rem(z + o, cols)), device_id_type=MESH,
        )
        for o in range(1, cols)
    ]
    for copy in stat_copies:
        copy.start()
    for copy in stat_copies:
        copy.wait()
    means = stats[:, 0:1, :]
    mean_all = jnp.sum(means, axis=0) * (1.0 / cols)
    spread = means - mean_all[None]
    squares = jnp.sum(stats[:, 1:2, :] + width * (spread * spread), axis=0)
    scale_all = lax.rsqrt(squares * (1.0 / (width * cols)) + 1e-06)
    for kind in range(2):
        lanes = slice(kind * both, (kind + 1) * both)
        line = lax.broadcasted_iota(jnp.int32, (128, both), 0)
        tile = jnp.transpose(jnp.where(line == 0, mean_all[:, lanes], scale_all[:, lanes]))
        x = raw[kind].reshape(both, width).astype(F32)
        normed = (x - tile[:, 0:1]) * tile[:, 1:2] * gain_ref[...]
        nrm[kind * both : (kind + 1) * both, :] = normed.astype(BF16)
        if kind == 0:
            nrm_t[...] = jnp.transpose(normed).astype(BF16)

    acc[...] = jnp.zeros_like(acc)
    sal[...] = jnp.zeros_like(sal)

    def to_right_copy(c):
        return pltpu.make_async_remote_copy(
            src_ref=to_right.at[c], dst_ref=from_left.at[c],
            send_sem=right_send.at[c], recv_sem=right_recv.at[c],
            device_id=at_col(lax.rem(z + 1, cols)), device_id_type=MESH,
        )

    def to_left_copy(c):
        return pltpu.make_async_remote_copy(
            src_ref=to_left.at[c], dst_ref=from_right.at[c],
            send_sem=left_send.at[c], recv_sem=left_recv.at[c],
            device_id=at_col(lax.rem(z + cols - 1, cols)), device_id_type=MESH,
        )

    def make_part(c):
        win_copy(c).wait()
        wout_copy(c).wait()
        part[c, 0 : 2 * both, :] = dot(nrm[...], win[c])
        part[c, 2 * both :, :] = dot(gy[...].reshape(both, width), wout[c], ((1,), (1,)))

    def finish(c):
        total = part[c] + from_left[c].astype(F32) + from_right[c].astype(F32)
        index = dp * nch + c
        pre = total[0 : 2 * both] + bin_ref[pl.ds(index, 1), :]
        cdf = 0.5 * (1.0 + lax.erf(pre * 0.7071067811865476))
        act = pre * cdf
        pre_f = pre[0:both]
        slope = cdf[0:both] + pre_f * jnp.exp(-0.5 * pre_f * pre_f) * 0.3989422804014327
        grad_pre = (total[2 * both :] * slope).astype(BF16)
        act_ft = jnp.transpose(act[0:both]).astype(BF16)
        masked = (act[both:] * keep_ref[pl.ds(index, 1), :]).astype(BF16)
        step = min(width, 512)
        term = jnp.zeros((8, CHUNK), F32)
        lanes_sum = jnp.zeros((CHUNK, 128), F32)
        for k in range(0, width, step):
            span = slice(k, min(k + step, width))
            grad = dot(nrm_t[span, :], grad_pre)
            prod = jnp.abs(win[c, span, :].astype(F32) * grad)
            term = term + jnp.sum(prod.reshape(-1, 8, CHUNK), axis=0)
            grad = dot(act_ft, gy[:, :, span].reshape(both, -1))
            prod = jnp.abs(wout[c, :, span].astype(F32) * grad)
            for q in range(0, prod.shape[1], 128):
                lanes_sum = lanes_sum + prod[:, q : q + 128]
            acc[:, span] += dot(masked, wout[c, :, span])
        total_term = jnp.sum(term, axis=0, keepdims=True) + jnp.sum(
            jnp.transpose(lanes_sum), axis=0, keepdims=True
        )
        sal[pl.ds(c, 1), :] = total_term

    make_part(0)

    def step(s, carry):
        c_right = s - LAG * z
        c_left = s - LAG * (cols - 1 - z)
        c_done = s - LAG * jnp.maximum(z, cols - 1 - z)

        @pl.when((c_right >= 0) & (c_right < nch))
        def _():
            c = c_right

            @pl.when(z > 0)
            def _():
                to_right_copy(c).wait_recv()

            @pl.when(z == 0)
            def _():
                from_left[c] = jnp.zeros(from_left.shape[1:], BF16)

            @pl.when(z < cols - 1)
            def _():
                to_right[c] = (part[c] + from_left[c].astype(F32)).astype(BF16)
                to_right_copy(c).start()

        @pl.when((c_left >= 0) & (c_left < nch))
        def _():
            c = c_left

            @pl.when(z < cols - 1)
            def _():
                to_left_copy(c).wait_recv()

            @pl.when(z == cols - 1)
            def _():
                from_right[c] = jnp.zeros(from_right.shape[1:], BF16)

            @pl.when(z > 0)
            def _():
                to_left[c] = (part[c] + from_right[c].astype(F32)).astype(BF16)
                to_left_copy(c).start()

        @pl.when(s + 1 < nch)
        def _():
            make_part(s + 1)

        @pl.when((c_done >= 0) & (c_done < nch))
        def _():
            finish(c_done)

        return carry

    lax.fori_loop(0, nch + LAG * (cols - 1), step, 0)

    sal_all[z] = sal[...]
    sal_copies = [
        pltpu.make_async_remote_copy(
            src_ref=sal_all.at[z], dst_ref=sal_all.at[z],
            send_sem=sal_send.at[o - 1], recv_sem=sal_recv.at[o - 1],
            device_id=at_col(lax.rem(z + o, cols)), device_id_type=MESH,
        )
        for o in range(1, cols)
    ]
    for copy in sal_copies:
        copy.start()

    half_copy = pltpu.make_async_remote_copy(
        src_ref=acc.at[pl.ds(pl.multiple_of(other * tokens, tokens), tokens), :],
        dst_ref=half, send_sem=half_send, recv_sem=half_recv,
        device_id=at_dp(other), device_id_type=MESH,
    )
    half_copy.start()
    half_copy.wait()
    share = tokens // rows
    here = acc[pl.ds(pl.multiple_of(dp * tokens, tokens), tokens), :] + half[...]
    mine[...] = here.astype(BF16)

    def share_of(r):
        return pl.ds(pl.multiple_of(r * share, share), share)

    blk_copies = [
        pltpu.make_async_remote_copy(
            src_ref=mine.at[share_of(lax.rem(row + o, rows)), :], dst_ref=blocks.at[o - 1],
            send_sem=blk_send.at[o - 1], recv_sem=blk_recv.at[o - 1],
            device_id=at_row(lax.rem(row + o, rows)), device_id_type=MESH,
        )
        for o in range(1, rows)
    ]
    for copy in blk_copies:
        copy.start()

    for copy in sal_copies:
        copy.wait()
    sal_fin[dp] = jnp.sum(sal_all[...], axis=0) * (1.0 / (width * cols))
    fin_copy = pltpu.make_async_remote_copy(
        src_ref=sal_fin.at[dp], dst_ref=sal_fin.at[dp], send_sem=fin_send, recv_sem=fin_recv,
        device_id=at_dp(other), device_id_type=MESH,
    )
    fin_copy.start()

    result = acc[share_of(dp * rows + row), :] + half[share_of(row), :] + bout_ref[...]
    for o, copy in enumerate(blk_copies):
        copy.wait()
        result = result + blocks[o].astype(F32)
    ret_out[...] = result.astype(BF16)
    fin_copy.wait()
    sal_out[...] = sal_fin[...]

    @pl.loop(0, nch)
    def _(c):
        @pl.when(z < cols - 1)
        def _():
            to_right_copy(c).wait_send()

        @pl.when(z > 0)
        def _():
            to_left_copy(c).wait_send()


def local(
    cols, rows,
    forget_tokens, forget_cotangent, forget_labels, retain_tokens, ln_gain,
    w_in, b_in, w_out, b_out, pruned,
):
    tokens, width = forget_tokens.shape
    neurons = w_in.shape[1]
    nch = neurons // 2 // CHUNK
    pad = -(-nch // 8) * 8
    both = 2 * tokens
    grad_y = forget_cotangent * forget_labels[:, None].astype(BF16)
    ids = lax.axis_index("row") * neurons + jnp.arange(neurons, dtype=jnp.int32)
    is_pruned = jnp.any(pruned[:, None] == ids[None, :], axis=0)
    keep = jnp.where(is_pruned, 0.0, 1.0).astype(F32).reshape(2 * nch, CHUNK)
    line = (nch, 3 * both, CHUNK)
    dma = pltpu.SemaphoreType.DMA
    anywhere = pl.BlockSpec(memory_space=pl.ANY)
    vmem = pl.BlockSpec(memory_space=pltpu.VMEM)
    macs = both * width * (neurons // 2) * 6
    saliency, retain_out = pl.pallas_call(
        functools.partial(kernel, (cols, rows, tokens, nch)),
        out_shape=(
            jax.ShapeDtypeStruct((2, pad, CHUNK), F32),
            jax.ShapeDtypeStruct((tokens // rows, width), BF16),
        ),
        in_specs=[anywhere] * 5 + [vmem] * 4,
        out_specs=(vmem, vmem),
        scratch_shapes=[
            pltpu.VMEM((2, 2, tokens, width), BF16),
            pltpu.VMEM((2, tokens, width), BF16),
            pltpu.VMEM((2 * both, width), BF16),
            pltpu.VMEM((width, both), BF16),
            pltpu.VMEM((cols, 8, 2 * both), F32),
            pltpu.VMEM((nch, width, CHUNK), BF16),
            pltpu.VMEM((nch, CHUNK, width), BF16),
            pltpu.VMEM(line, F32),
            pltpu.VMEM(line, BF16),
            pltpu.VMEM(line, BF16),
            pltpu.VMEM(line, BF16),
            pltpu.VMEM(line, BF16),
            pltpu.VMEM((both, width), F32),
            pltpu.VMEM((tokens, width), F32),
            pltpu.VMEM((rows - 1, tokens // rows, width), BF16),
            pltpu.VMEM((tokens, width), BF16),
            pltpu.VMEM((pad, CHUNK), F32),
            pltpu.VMEM((cols, pad, CHUNK), F32),
            pltpu.VMEM((2, pad, CHUNK), F32),
            dma((3,)), dma((3,)), dma((3,)),
            dma((cols - 1,)), dma((cols - 1,)),
            dma((nch,)), dma((nch,)),
            dma((nch,)), dma((nch,)), dma((nch,)), dma((nch,)),
            dma(()), dma(()),
            dma((rows - 1,)), dma((rows - 1,)),
            dma((cols - 1,)), dma((cols - 1,)),
            dma(()), dma(()),
        ],
        compiler_params=pltpu.CompilerParams(
            collective_id=0, has_side_effects=True, vmem_limit_bytes=62 * 2**20
        ),
        cost_estimate=pl.CostEstimate(
            flops=2 * macs, bytes_accessed=2 * width * neurons, transcendentals=0
        ),
        name="unlearn_step",
    )(
        forget_tokens, retain_tokens, grad_y, w_in, w_out,
        ln_gain[None, :], b_in.reshape(2 * nch, CHUNK), keep, b_out[None, :],
    )
    return (saliency[:, :nch].reshape(neurons), retain_out)


def solution(mesh):
    in_specs = (
        P("dp", "col"),
        P("dp", "col"),
        P("dp"),
        P("dp", "col"),
        P("col"),
        P("col", "row"),
        P("row"),
        P("row", "col"),
        P("col"),
        P("row"),
    )
    out_specs = (P("row"), P(("dp", "row"), "col"))
    body = functools.partial(local, mesh.shape["col"], mesh.shape["row"])
    return jax.shard_map(body, mesh=mesh, in_specs=in_specs, out_specs=out_specs, check_vma=False)
```

```python
import functools

import jax
import jax.numpy as jnp
from jax import lax
from jax.experimental import pallas as pl
from jax.experimental.pallas import tpu as pltpu
from jax.sharding import PartitionSpec as P

F32, BF16 = jnp.float32, jnp.bfloat16
MESH = pl.DeviceIdType.MESH
CHUNK = 128
SLOTS = 160
LAG = 2


def dot(left, right, contract=((1,), (0,))):
    return lax.dot_general(left, right, (contract, ((), ())), preferred_element_type=F32)


def column(values):
    n = values.shape[1]
    return jnp.transpose(jnp.broadcast_to(values, (128, n)))[:, 0:1]


def prepare(
    sizes,
    ft_hbm, rt_hbm, ct_hbm, lab_ref, gain_ref,
    nrm, nrm_t, gy, count,
    raw, cot, lab, stats,
    raw_loc, raw_send, raw_recv, st_send, st_recv,
):
    cols, tokens = sizes
    width = nrm.shape[1]
    both = 2 * tokens
    dp, row, z = lax.axis_index("dp"), lax.axis_index("row"), lax.axis_index("col")
    other = 1 - dp
    sources = (ft_hbm, rt_hbm, ct_hbm)
    places = (raw.at[0, dp], raw.at[1, dp], cot.at[dp])
    own = [
        pltpu.make_async_copy(src, dst, raw_loc.at[i])
        for i, (src, dst) in enumerate(zip(sources, places))
    ]
    for copy in own:
        copy.start()
    lab[dp] = jnp.broadcast_to(lab_ref[...].astype(F32)[None, :], lab.shape[1:])

    barrier = pltpu.get_barrier_semaphore()
    pl.semaphore_signal(barrier, inc=1, device_id=(other, row, z), device_id_type=MESH)
    for o in range(1, cols):
        pl.semaphore_signal(
            barrier, inc=1, device_id=(dp, row, lax.rem(z + o, cols)), device_id_type=MESH
        )
    pl.semaphore_wait(barrier, cols)

    swaps = [
        pltpu.make_async_remote_copy(
            src_ref=src, dst_ref=dst, send_sem=raw_send.at[i], recv_sem=raw_recv.at[i],
            device_id=(other, row, z), device_id_type=MESH,
        )
        for i, (src, dst) in enumerate(
            zip(sources + (lab.at[dp],), places + (lab.at[dp],))
        )
    ]
    for copy in swaps:
        copy.start()
    for copy in own:
        copy.wait()

    def own_stats(d):
        for kind in range(2):
            x = raw[kind, d].astype(F32)
            mean_here = jnp.sum(x, axis=1, keepdims=True) * (1.0 / width)
            cent = x - mean_here
            square = jnp.sum(cent * cent, axis=1, keepdims=True)
            lane = lax.broadcasted_iota(jnp.int32, (tokens, 128), 1)
            tile = jnp.where(lane == 0, mean_here, square)
            stats[z, 2 * kind + d] = jnp.transpose(tile)[0:8, :]

    own_stats(dp)
    for copy in swaps:
        copy.wait()
    own_stats(other)
    stat_copies = [
        pltpu.make_async_remote_copy(
            src_ref=stats.at[z], dst_ref=stats.at[z],
            send_sem=st_send.at[o - 1], recv_sem=st_recv.at[o - 1],
            device_id=(dp, row, lax.rem(z + o, cols)), device_id_type=MESH,
        )
        for o in range(1, cols)
    ]
    for copy in stat_copies:
        copy.start()

    labels = jnp.concatenate([lab[0][0:1], lab[1][0:1]], axis=1)
    at = lax.broadcasted_iota(jnp.int32, (both, both), 0)
    to = lax.broadcasted_iota(jnp.int32, (both, both), 1)
    until = jnp.where(at <= to, 1.0, 0.0).astype(BF16)
    ranks = dot(jnp.broadcast_to(labels, (16, both)).astype(BF16), until)[0:1]
    spot = jnp.where(labels > 0.5, ranks - 1.0, -1.0)
    select = jnp.where(at.astype(F32) == spot, 1.0, 0.0).astype(BF16)
    count[...] = jnp.broadcast_to(jnp.sum(labels, axis=1, keepdims=True), count.shape)
    gy[...] = dot(select, cot[...].reshape(both, width)).astype(BF16)

    for copy in stat_copies:
        copy.wait()
    gain = gain_ref[...][None, :]
    for kind in range(2):
        scaled = []
        for d in range(2):
            here = stats[:, 2 * kind + d]
            means = here[:, 0:1, :]
            mean_all = jnp.sum(means, axis=0) * (1.0 / cols)
            spread = means - mean_all[None]
            squares = jnp.sum(here[:, 1:2, :] + width * (spread * spread), axis=0)
            scale = lax.rsqrt(squares * (1.0 / (width * cols)) + 1e-06)
            x = raw[kind, d].astype(F32)
            scaled.append(((x - column(mean_all)) * column(scale) * gain).astype(BF16))
        normed = jnp.concatenate(scaled, axis=0)
        if kind == 0:
            chosen = dot(select, normed)
            nrm[0:both, :] = chosen.astype(BF16)
            nrm_t[...] = jnp.transpose(chosen).astype(BF16)
        else:
            nrm[both : 2 * both, :] = normed


def kernel(
    sizes,
    win_hbm, wout_hbm, nrm, nrm_t, gy, bin_ref, pruned_ref, bout_ref,
    sal_out, ret_out,
    win, wout, part, from_left, from_right, to_right, to_left,
    acc, half, blocks, mine, sal, sal_all, sal_fin,
    win_sem, wout_sem,
    right_send, right_recv, left_send, left_recv,
    half_send, half_recv, blk_send, blk_recv, sal_send, sal_recv, fin_send, fin_recv,
):
    cols, rows, tokens, nch, slots = sizes
    width = nrm.shape[1]
    both = 2 * tokens
    dp, row, z = lax.axis_index("dp"), lax.axis_index("row"), lax.axis_index("col")
    other = 1 - dp
    end_f, end_r = slots, slots + both

    def at_dp(d):
        return (d, row, z)

    def at_row(r):
        return (dp, r, z)

    def at_col(c):
        return (dp, row, c)

    def win_copy(c):
        lanes = pl.ds(pl.multiple_of((dp * nch + c) * CHUNK, CHUNK), CHUNK)
        return pltpu.make_async_copy(win_hbm.at[:, lanes], win.at[c], win_sem.at[c])

    def wout_copy(c):
        lines = pl.ds(pl.multiple_of((dp * nch + c) * CHUNK, CHUNK), CHUNK)
        return pltpu.make_async_copy(wout_hbm.at[lines, :], wout.at[c], wout_sem.at[c])

    @pl.loop(0, nch)
    def _(c):
        win_copy(c).start()
        wout_copy(c).start()

    barrier = pltpu.get_barrier_semaphore()
    pl.semaphore_signal(barrier, inc=1, device_id=at_dp(other), device_id_type=MESH)
    for o in range(1, cols):
        pl.semaphore_signal(
            barrier, inc=1, device_id=at_col(lax.rem(z + o, cols)), device_id_type=MESH
        )
    for o in range(1, rows):
        pl.semaphore_signal(
            barrier, inc=1, device_id=at_row(lax.rem(row + o, rows)), device_id_type=MESH
        )
    pl.semaphore_wait(barrier, 1 + (cols - 1) + (rows - 1))

    pruned = column(pruned_ref[...].astype(F32)[None, :])
    lane_ids = lax.broadcasted_iota(jnp.int32, (1, CHUNK), 1)
    acc[...] = jnp.zeros_like(acc)
    sal[...] = jnp.zeros_like(sal)

    def to_right_copy(c):
        return pltpu.make_async_remote_copy(
            src_ref=to_right.at[c], dst_ref=from_left.at[c],
            send_sem=right_send.at[c], recv_sem=right_recv.at[c],
            device_id=at_col(lax.rem(z + 1, cols)), device_id_type=MESH,
        )

    def to_left_copy(c):
        return pltpu.make_async_remote_copy(
            src_ref=to_left.at[c], dst_ref=from_right.at[c],
            send_sem=left_send.at[c], recv_sem=left_recv.at[c],
            device_id=at_col(lax.rem(z + cols - 1, cols)), device_id_type=MESH,
        )

    def make_part(c):
        win_copy(c).wait()
        wout_copy(c).wait()
        part[c, 0:end_f, :] = dot(nrm[0:slots, :], win[c])
        part[c, end_f:end_r, :] = dot(nrm[both : 2 * both, :], win[c])
        part[c, end_r:, :] = dot(gy[0:slots, :], wout[c], ((1,), (1,)))

    def finish(c):
        total = part[c] + from_left[c].astype(F32) + from_right[c].astype(F32)
        first = pl.multiple_of((dp * nch + c) * CHUNK, CHUNK)
        pre = total[0:end_r] + bin_ref[pl.ds(first, CHUNK)][None, :]
        cdf = 0.5 * (1.0 + lax.erf(pre * 0.7071067811865476))
        act = pre * cdf
        pre_f = pre[0:slots]
        slope = cdf[0:slots] + pre_f * jnp.exp(-0.5 * pre_f * pre_f) * 0.3989422804014327
        grad_pre, act_f = total[end_r:] * slope, act[0:slots]
        if slots < both:
            rest = jnp.zeros((both - slots, CHUNK), F32)
            grad_pre = jnp.concatenate([grad_pre, rest], axis=0)
            act_f = jnp.concatenate([act_f, rest], axis=0)
        grad_pre = grad_pre.astype(BF16)
        act_ft = jnp.transpose(act_f).astype(BF16)
        ids = (lane_ids + (row * (2 * nch * CHUNK) + first)).astype(F32)
        hits = jnp.max(jnp.where(pruned == ids, 1.0, 0.0), axis=0, keepdims=True)
        masked = (act[slots:] * (1.0 - hits)).astype(BF16)
        step = min(width, 512)
        term = jnp.zeros((8, CHUNK), F32)
        lanes_sum = jnp.zeros((CHUNK, 128), F32)
        for k in range(0, width, step):
            span = slice(k, min(k + step, width))
            grad = dot(nrm_t[span, :], grad_pre)
            prod = jnp.abs(win[c, span, :].astype(F32) * grad)
            term = term + jnp.sum(prod.reshape(-1, 8, CHUNK), axis=0)
            grad = dot(act_ft, gy[:, span])
            prod = jnp.abs(wout[c, :, span].astype(F32) * grad)
            for q in range(0, prod.shape[1], 128):
                lanes_sum = lanes_sum + prod[:, q : q + 128]
            acc[:, span] += dot(masked, wout[c, :, span])
        total_term = jnp.sum(term, axis=0, keepdims=True) + jnp.sum(
            jnp.transpose(lanes_sum), axis=0, keepdims=True
        )
        sal[pl.ds(c, 1), :] = total_term

    make_part(0)

    def step(s, carry):
        c_right = s - LAG * z
        c_left = s - LAG * (cols - 1 - z)
        c_done = s - LAG * jnp.maximum(z, cols - 1 - z)

        @pl.when((c_right >= 0) & (c_right < nch))
        def _():
            c = c_right

            @pl.when(z > 0)
            def _():
                to_right_copy(c).wait_recv()

            @pl.when(z == 0)
            def _():
                from_left[c] = jnp.zeros(from_left.shape[1:], BF16)

            @pl.when(z < cols - 1)
            def _():
                to_right[c] = (part[c] + from_left[c].astype(F32)).astype(BF16)
                to_right_copy(c).start()

        @pl.when((c_left >= 0) & (c_left < nch))
        def _():
            c = c_left

            @pl.when(z < cols - 1)
            def _():
                to_left_copy(c).wait_recv()

            @pl.when(z == cols - 1)
            def _():
                from_right[c] = jnp.zeros(from_right.shape[1:], BF16)

            @pl.when(z > 0)
            def _():
                to_left[c] = (part[c] + from_right[c].astype(F32)).astype(BF16)
                to_left_copy(c).start()

        @pl.when(s + 1 < nch)
        def _():
            make_part(s + 1)

        @pl.when((c_done >= 0) & (c_done < nch))
        def _():
            finish(c_done)

        return carry

    lax.fori_loop(0, nch + LAG * (cols - 1), step, 0)

    sal_all[z] = sal[...]
    sal_copies = [
        pltpu.make_async_remote_copy(
            src_ref=sal_all.at[z], dst_ref=sal_all.at[z],
            send_sem=sal_send.at[o - 1], recv_sem=sal_recv.at[o - 1],
            device_id=at_col(lax.rem(z + o, cols)), device_id_type=MESH,
        )
        for o in range(1, cols)
    ]
    for copy in sal_copies:
        copy.start()

    half_copy = pltpu.make_async_remote_copy(
        src_ref=acc.at[pl.ds(pl.multiple_of(other * tokens, tokens), tokens), :],
        dst_ref=half, send_sem=half_send, recv_sem=half_recv,
        device_id=at_dp(other), device_id_type=MESH,
    )
    half_copy.start()
    half_copy.wait()
    share = tokens // rows
    here = acc[pl.ds(pl.multiple_of(dp * tokens, tokens), tokens), :] + half[...]
    mine[...] = here.astype(BF16)

    def share_of(r):
        return pl.ds(pl.multiple_of(r * share, share), share)

    blk_copies = [
        pltpu.make_async_remote_copy(
            src_ref=mine.at[share_of(lax.rem(row + o, rows)), :], dst_ref=blocks.at[o - 1],
            send_sem=blk_send.at[o - 1], recv_sem=blk_recv.at[o - 1],
            device_id=at_row(lax.rem(row + o, rows)), device_id_type=MESH,
        )
        for o in range(1, rows)
    ]
    for copy in blk_copies:
        copy.start()

    for copy in sal_copies:
        copy.wait()
    sal_fin[dp] = jnp.sum(sal_all[...], axis=0) * (1.0 / (width * cols))
    fin_copy = pltpu.make_async_remote_copy(
        src_ref=sal_fin.at[dp], dst_ref=sal_fin.at[dp], send_sem=fin_send, recv_sem=fin_recv,
        device_id=at_dp(other), device_id_type=MESH,
    )
    fin_copy.start()

    result = acc[share_of(dp * rows + row), :] + half[share_of(row), :] + bout_ref[...][None, :]
    for o, copy in enumerate(blk_copies):
        copy.wait()
        result = result + blocks[o].astype(F32)
    ret_out[...] = result.astype(BF16)
    fin_copy.wait()
    sal_out[...] = sal_fin[...]

    @pl.loop(0, nch)
    def _(c):
        @pl.when(z < cols - 1)
        def _():
            to_right_copy(c).wait_send()

        @pl.when(z > 0)
        def _():
            to_left_copy(c).wait_send()


def local(
    cols, rows,
    forget_tokens, forget_cotangent, forget_labels, retain_tokens, ln_gain,
    w_in, b_in, w_out, b_out, pruned,
):
    tokens, width = forget_tokens.shape
    neurons = w_in.shape[1]
    nch = neurons // 2 // CHUNK
    pad = -(-nch // 8) * 8
    both = 2 * tokens
    dma = pltpu.SemaphoreType.DMA
    anywhere = pl.BlockSpec(memory_space=pl.ANY)
    vmem = pl.BlockSpec(memory_space=pltpu.VMEM)
    nrm, nrm_t, gy, count = pl.pallas_call(
        functools.partial(prepare, (cols, tokens)),
        out_shape=(
            jax.ShapeDtypeStruct((2 * both, width), BF16),
            jax.ShapeDtypeStruct((width, both), BF16),
            jax.ShapeDtypeStruct((both, width), BF16),
            jax.ShapeDtypeStruct((8, 128), F32),
        ),
        in_specs=[anywhere] * 3 + [vmem] * 2,
        out_specs=(vmem,) * 4,
        scratch_shapes=[
            pltpu.VMEM((2, 2, tokens, width), BF16),
            pltpu.VMEM((2, tokens, width), BF16),
            pltpu.VMEM((2, 8, tokens), F32),
            pltpu.VMEM((cols, 4, 8, tokens), F32),
            dma((3,)), dma((4,)), dma((4,)),
            dma((cols - 1,)), dma((cols - 1,)),
        ],
        compiler_params=pltpu.CompilerParams(
            collective_id=0, has_side_effects=True, vmem_limit_bytes=62 * 2**20
        ),
        name="prepare",
    )(forget_tokens, retain_tokens, forget_cotangent, forget_labels, ln_gain)

    def stream(slots, collective_id):
        line = (nch, 2 * slots + both, CHUNK)
        macs = 3 * (slots + both) * width * (neurons // 2)
        return pl.pallas_call(
            functools.partial(kernel, (cols, rows, tokens, nch, slots)),
            out_shape=(
                jax.ShapeDtypeStruct((2, pad, CHUNK), F32),
                jax.ShapeDtypeStruct((tokens // rows, width), BF16),
            ),
            in_specs=[anywhere] * 2 + [vmem] * 6,
            out_specs=(vmem, vmem),
            scratch_shapes=[
                pltpu.VMEM((nch, width, CHUNK), BF16),
                pltpu.VMEM((nch, CHUNK, width), BF16),
                pltpu.VMEM(line, F32),
                pltpu.VMEM(line, BF16),
                pltpu.VMEM(line, BF16),
                pltpu.VMEM(line, BF16),
                pltpu.VMEM(line, BF16),
                pltpu.VMEM((both, width), F32),
                pltpu.VMEM((tokens, width), F32),
                pltpu.VMEM((rows - 1, tokens // rows, width), BF16),
                pltpu.VMEM((tokens, width), BF16),
                pltpu.VMEM((pad, CHUNK), F32),
                pltpu.VMEM((cols, pad, CHUNK), F32),
                pltpu.VMEM((2, pad, CHUNK), F32),
                dma((nch,)), dma((nch,)),
                dma((nch,)), dma((nch,)), dma((nch,)), dma((nch,)),
                dma(()), dma(()),
                dma((rows - 1,)), dma((rows - 1,)),
                dma((cols - 1,)), dma((cols - 1,)),
                dma(()), dma(()),
            ],
            compiler_params=pltpu.CompilerParams(
                collective_id=collective_id, has_side_effects=True, vmem_limit_bytes=62 * 2**20
            ),
            cost_estimate=pl.CostEstimate(
                flops=2 * macs, bytes_accessed=2 * width * neurons, transcendentals=0
            ),
            name="stream_%d" % slots,
        )

    rest = (w_in, w_out, nrm, nrm_t, gy, b_in, pruned, b_out)
    few = SLOTS * both // 256
    saliency, retain_out = lax.cond(
        count[0, 0] <= few,
        lambda args: tuple(stream(few, 1)(*args)),
        lambda args: tuple(stream(both, 2)(*args)),
        rest,
    )
    return (saliency[:, :nch].reshape(neurons), retain_out)


def solution(mesh):
    in_specs = (
        P("dp", "col"),
        P("dp", "col"),
        P("dp"),
        P("dp", "col"),
        P("col"),
        P("col", "row"),
        P("row"),
        P("row", "col"),
        P("col"),
        P("row"),
    )
    out_specs = (P("row"), P(("dp", "row"), "col"))
    body = functools.partial(local, mesh.shape["col"], mesh.shape["row"])
    return jax.shard_map(body, mesh=mesh, in_specs=in_specs, out_specs=out_specs, check_vma=False)
```

```python
import functools

import jax
import jax.numpy as jnp
from jax import lax
from jax.experimental import pallas as pl
from jax.experimental.pallas import tpu as pltpu
from jax.sharding import PartitionSpec as P

F32, BF16 = jnp.float32, jnp.bfloat16
MESH = pl.DeviceIdType.MESH
CHUNK = 128
SLOTS = (128, 144, 160)
LEAD = 6
LAG = 2


def dot(left, right, contract=((1,), (0,))):
    return lax.dot_general(left, right, (contract, ((), ())), preferred_element_type=F32)


def column(values):
    n = values.shape[1]
    return jnp.transpose(jnp.broadcast_to(values, (128, n)))[:, 0:1]


def prepare(sizes, ct_hbm, lab_ref, gy, select, count, cot, lab, loc_sem, send_sem, recv_sem):
    tokens, width = sizes
    both = 2 * tokens
    dp, row, z = lax.axis_index("dp"), lax.axis_index("row"), lax.axis_index("col")
    other = 1 - dp
    own = pltpu.make_async_copy(ct_hbm, cot.at[dp], loc_sem)
    own.start()
    lab[dp] = jnp.broadcast_to(lab_ref[...].astype(F32)[None, :], lab.shape[1:])
    barrier = pltpu.get_barrier_semaphore()
    pl.semaphore_signal(barrier, inc=1, device_id=(other, row, z), device_id_type=MESH)
    pl.semaphore_wait(barrier, 1)
    swaps = [
        pltpu.make_async_remote_copy(
            src_ref=src, dst_ref=dst, send_sem=send_sem.at[i], recv_sem=recv_sem.at[i],
            device_id=(other, row, z), device_id_type=MESH,
        )
        for i, (src, dst) in enumerate(((lab.at[dp], lab.at[dp]), (ct_hbm, cot.at[dp])))
    ]
    for copy in swaps:
        copy.start()
    swaps[0].wait()
    labels = jnp.concatenate([lab[0][0:1], lab[1][0:1]], axis=1)
    at = lax.broadcasted_iota(jnp.int32, (both, both), 0)
    to = lax.broadcasted_iota(jnp.int32, (both, both), 1)
    until = jnp.where(at <= to, 1.0, 0.0).astype(BF16)
    ranks = dot(jnp.broadcast_to(labels, (16, both)).astype(BF16), until)[0:1]
    spot = jnp.where(labels > 0.5, ranks - 1.0, -1.0)
    select[...] = jnp.where(at.astype(F32) == spot, 1.0, 0.0).astype(BF16)
    count[...] = jnp.broadcast_to(jnp.sum(labels, axis=1, keepdims=True), count.shape)
    own.wait()
    swaps[1].wait()
    gy[...] = dot(select[...], cot[...].reshape(both, width)).astype(BF16)


def kernel(
    sizes,
    ft_hbm, rt_hbm, win_hbm, wout_hbm, gy, select, gain_ref, bin_ref, pruned_ref, bout_ref,
    sal_out, ret_out,
    raw, nrm, nrm_t, stats, win, wout, part, from_left, from_right, to_right, to_left,
    acc, half, blocks, mine, sal, sal_all, sal_fin,
    raw_loc, raw_send, raw_recv, st_send, st_recv, win_sem, wout_sem,
    right_send, right_recv, left_send, left_recv,
    half_send, half_recv, blk_send, blk_recv, sal_send, sal_recv, fin_send, fin_recv,
):
    cols, rows, tokens, nch, slots = sizes
    width = nrm.shape[1]
    both = 2 * tokens
    dp, row, z = lax.axis_index("dp"), lax.axis_index("row"), lax.axis_index("col")
    other = 1 - dp
    end_f, end_r = slots, slots + both

    def at_dp(d):
        return (d, row, z)

    def at_row(r):
        return (dp, r, z)

    def at_col(c):
        return (dp, row, c)

    def win_copy(c):
        lanes = pl.ds(pl.multiple_of((dp * nch + c) * CHUNK, CHUNK), CHUNK)
        return pltpu.make_async_copy(win_hbm.at[:, lanes], win.at[c], win_sem.at[c])

    def wout_copy(c):
        lines = pl.ds(pl.multiple_of((dp * nch + c) * CHUNK, CHUNK), CHUNK)
        return pltpu.make_async_copy(wout_hbm.at[lines, :], wout.at[c], wout_sem.at[c])

    sources = (ft_hbm, rt_hbm)
    own = [
        pltpu.make_async_copy(src, raw.at[i, dp], raw_loc.at[i]) for i, src in enumerate(sources)
    ]
    wout_copy(0).start()
    for copy in own:
        copy.start()

    @pl.loop(1, nch)
    def _(c):
        wout_copy(c).start()

    @pl.loop(0, nch)
    def _(c):
        win_copy(c).start()

    barrier = pltpu.get_barrier_semaphore()
    pl.semaphore_signal(barrier, inc=1, device_id=at_dp(other), device_id_type=MESH)
    for o in range(1, cols):
        pl.semaphore_signal(
            barrier, inc=1, device_id=at_col(lax.rem(z + o, cols)), device_id_type=MESH
        )
    for o in range(1, rows):
        pl.semaphore_signal(
            barrier, inc=1, device_id=at_row(lax.rem(row + o, rows)), device_id_type=MESH
        )
    pl.semaphore_wait(barrier, 1 + (cols - 1) + (rows - 1))

    swaps = [
        pltpu.make_async_remote_copy(
            src_ref=src, dst_ref=raw.at[i, dp], send_sem=raw_send.at[i], recv_sem=raw_recv.at[i],
            device_id=at_dp(other), device_id_type=MESH,
        )
        for i, src in enumerate(sources)
    ]
    for copy in swaps:
        copy.start()
    stat_copies = [
        pltpu.make_async_remote_copy(
            src_ref=stats.at[z], dst_ref=stats.at[z],
            send_sem=st_send.at[o - 1], recv_sem=st_recv.at[o - 1],
            device_id=at_col(lax.rem(z + o, cols)), device_id_type=MESH,
        )
        for o in range(1, cols)
    ]

    def measure_tokens():
        for copy in own + swaps:
            copy.wait()
        for kind in range(2):
            for d in range(2):
                x = raw[kind, d].astype(F32)
                mean_here = jnp.sum(x, axis=1, keepdims=True) * (1.0 / width)
                cent = x - mean_here
                square = jnp.sum(cent * cent, axis=1, keepdims=True)
                lane = lax.broadcasted_iota(jnp.int32, (tokens, 128), 1)
                tile = jnp.where(lane == 0, mean_here, square)
                stats[z, 2 * kind + d] = jnp.transpose(tile)[0:8, :]
        for copy in stat_copies:
            copy.start()

    def normalise():
        for copy in stat_copies:
            copy.wait()
        gain = gain_ref[...][None, :]
        for kind in range(2):
            scaled = []
            for d in range(2):
                here = stats[:, 2 * kind + d]
                means = here[:, 0:1, :]
                mean_all = jnp.sum(means, axis=0) * (1.0 / cols)
                spread = means - mean_all[None]
                squares = jnp.sum(here[:, 1:2, :] + width * (spread * spread), axis=0)
                scale = lax.rsqrt(squares * (1.0 / (width * cols)) + 1e-06)
                x = raw[kind, d].astype(F32)
                scaled.append(((x - column(mean_all)) * column(scale) * gain).astype(BF16))
            normed = jnp.concatenate(scaled, axis=0)
            if kind == 0:
                chosen = dot(select[...], normed)
                nrm[0:both, :] = chosen.astype(BF16)
                nrm_t[...] = jnp.transpose(chosen).astype(BF16)
            else:
                nrm[both : 2 * both, :] = normed

    pruned = column(pruned_ref[...].astype(F32)[None, :])
    lane_ids = lax.broadcasted_iota(jnp.int32, (1, CHUNK), 1)
    acc[...] = jnp.zeros_like(acc)
    sal[...] = jnp.zeros_like(sal)

    spans = (pl.ds(end_r, slots), pl.ds(0, end_r))

    def to_right_copy(k, c):
        return pltpu.make_async_remote_copy(
            src_ref=to_right.at[c, spans[k], :], dst_ref=from_left.at[c, spans[k], :],
            send_sem=right_send.at[k, c], recv_sem=right_recv.at[k, c],
            device_id=at_col(lax.rem(z + 1, cols)), device_id_type=MESH,
        )

    def to_left_copy(k, c):
        return pltpu.make_async_remote_copy(
            src_ref=to_left.at[c, spans[k], :], dst_ref=from_right.at[c, spans[k], :],
            send_sem=left_send.at[k, c], recv_sem=left_recv.at[k, c],
            device_id=at_col(lax.rem(z + cols - 1, cols)), device_id_type=MESH,
        )

    def make_grad(c):
        wout_copy(c).wait()
        part[c, end_r:, :] = dot(gy[0:slots, :], wout[c], ((1,), (1,)))

    def make_pre(c):
        win_copy(c).wait()
        part[c, 0:end_f, :] = dot(nrm[0:slots, :], win[c])
        part[c, end_f:end_r, :] = dot(nrm[both : 2 * both, :], win[c])

    def finish(c):
        total = part[c] + from_left[c].astype(F32) + from_right[c].astype(F32)
        first = pl.multiple_of((dp * nch + c) * CHUNK, CHUNK)
        pre = total[0:end_r] + bin_ref[pl.ds(first, CHUNK)][None, :]
        cdf = 0.5 * (1.0 + lax.erf(pre * 0.7071067811865476))
        act = pre * cdf
        pre_f = pre[0:slots]
        slope = cdf[0:slots] + pre_f * jnp.exp(-0.5 * pre_f * pre_f) * 0.3989422804014327
        grad_pre, act_f = total[end_r:] * slope, act[0:slots]
        if slots < both:
            rest = jnp.zeros((both - slots, CHUNK), F32)
            grad_pre = jnp.concatenate([grad_pre, rest], axis=0)
            act_f = jnp.concatenate([act_f, rest], axis=0)
        grad_pre = grad_pre.astype(BF16)
        act_ft = jnp.transpose(act_f).astype(BF16)
        ids = (lane_ids + (row * (2 * nch * CHUNK) + first)).astype(F32)
        hits = jnp.max(jnp.where(pruned == ids, 1.0, 0.0), axis=0, keepdims=True)
        masked = (act[slots:] * (1.0 - hits)).astype(BF16)
        step = min(width, 512)
        term = jnp.zeros((8, CHUNK), F32)
        lanes_sum = jnp.zeros((CHUNK, 128), F32)
        for k in range(0, width, step):
            span = slice(k, min(k + step, width))
            grad = dot(nrm_t[span, :], grad_pre)
            prod = jnp.abs(win[c, span, :].astype(F32) * grad)
            term = term + jnp.sum(prod.reshape(-1, 8, CHUNK), axis=0)
            grad = dot(act_ft, gy[:, span])
            prod = jnp.abs(wout[c, :, span].astype(F32) * grad)
            for q in range(0, prod.shape[1], 128):
                lanes_sum = lanes_sum + prod[:, q : q + 128]
            acc[:, span] += dot(masked, wout[c, :, span])
        total_term = jnp.sum(term, axis=0, keepdims=True) + jnp.sum(
            jnp.transpose(lanes_sum), axis=0, keepdims=True
        )
        sal[pl.ds(c, 1), :] = total_term

    make_grad(0)

    def forward(k, s):
        c_right = s - LAG * z
        c_left = s - LAG * (cols - 1 - z)
        span = spans[k]
        size = (span.size, CHUNK)

        @pl.when((c_right >= 0) & (c_right < nch))
        def _():
            c = c_right

            @pl.when(z > 0)
            def _():
                to_right_copy(k, c).wait_recv()

            @pl.when(z == 0)
            def _():
                from_left[c, span, :] = jnp.zeros(size, BF16)

            @pl.when(z < cols - 1)
            def _():
                total = part[c, span, :] + from_left[c, span, :].astype(F32)
                to_right[c, span, :] = total.astype(BF16)
                to_right_copy(k, c).start()

        @pl.when((c_left >= 0) & (c_left < nch))
        def _():
            c = c_left

            @pl.when(z < cols - 1)
            def _():
                to_left_copy(k, c).wait_recv()

            @pl.when(z == cols - 1)
            def _():
                from_right[c, span, :] = jnp.zeros(size, BF16)

            @pl.when(z > 0)
            def _():
                total = part[c, span, :] + from_right[c, span, :].astype(F32)
                to_left[c, span, :] = total.astype(BF16)
                to_left_copy(k, c).start()

    def step(s, carry):
        forward(0, s)
        forward(1, s - LEAD)

        @pl.when(s + 1 < nch)
        def _():
            make_grad(s + 1)

        @pl.when(s == 0)
        def _():
            measure_tokens()

        @pl.when(s == LEAD - 2)
        def _():
            normalise()

        ahead = s + 1 - LEAD

        @pl.when((ahead >= 0) & (ahead < nch))
        def _():
            make_pre(ahead)

        c_done = s - LEAD - LAG * jnp.maximum(z, cols - 1 - z)

        @pl.when((c_done >= 0) & (c_done < nch))
        def _():
            finish(c_done)

        return carry

    lax.fori_loop(0, nch + LEAD + LAG * (cols - 1), step, 0)

    sal_all[z] = sal[...]
    sal_copies = [
        pltpu.make_async_remote_copy(
            src_ref=sal_all.at[z], dst_ref=sal_all.at[z],
            send_sem=sal_send.at[o - 1], recv_sem=sal_recv.at[o - 1],
            device_id=at_col(lax.rem(z + o, cols)), device_id_type=MESH,
        )
        for o in range(1, cols)
    ]
    for copy in sal_copies:
        copy.start()

    half_copy = pltpu.make_async_remote_copy(
        src_ref=acc.at[pl.ds(pl.multiple_of(other * tokens, tokens), tokens), :],
        dst_ref=half, send_sem=half_send, recv_sem=half_recv,
        device_id=at_dp(other), device_id_type=MESH,
    )
    half_copy.start()
    half_copy.wait()
    share = tokens // rows
    here = acc[pl.ds(pl.multiple_of(dp * tokens, tokens), tokens), :] + half[...]
    mine[...] = here.astype(BF16)

    def share_of(r):
        return pl.ds(pl.multiple_of(r * share, share), share)

    blk_copies = [
        pltpu.make_async_remote_copy(
            src_ref=mine.at[share_of(lax.rem(row + o, rows)), :], dst_ref=blocks.at[o - 1],
            send_sem=blk_send.at[o - 1], recv_sem=blk_recv.at[o - 1],
            device_id=at_row(lax.rem(row + o, rows)), device_id_type=MESH,
        )
        for o in range(1, rows)
    ]
    for copy in blk_copies:
        copy.start()

    for copy in sal_copies:
        copy.wait()
    sal_fin[dp] = jnp.sum(sal_all[...], axis=0) * (1.0 / (width * cols))
    fin_copy = pltpu.make_async_remote_copy(
        src_ref=sal_fin.at[dp], dst_ref=sal_fin.at[dp], send_sem=fin_send, recv_sem=fin_recv,
        device_id=at_dp(other), device_id_type=MESH,
    )
    fin_copy.start()

    result = acc[share_of(dp * rows + row), :] + half[share_of(row), :] + bout_ref[...][None, :]
    for o, copy in enumerate(blk_copies):
        copy.wait()
        result = result + blocks[o].astype(F32)
    ret_out[...] = result.astype(BF16)
    fin_copy.wait()
    sal_out[...] = sal_fin[...]

    @pl.loop(0, nch)
    def _(c):
        @pl.when(z < cols - 1)
        def _():
            to_right_copy(0, c).wait_send()
            to_right_copy(1, c).wait_send()

        @pl.when(z > 0)
        def _():
            to_left_copy(0, c).wait_send()
            to_left_copy(1, c).wait_send()


def local(
    cols, rows,
    forget_tokens, forget_cotangent, forget_labels, retain_tokens, ln_gain,
    w_in, b_in, w_out, b_out, pruned,
):
    tokens, width = forget_tokens.shape
    neurons = w_in.shape[1]
    nch = neurons // 2 // CHUNK
    pad = -(-nch // 8) * 8
    both = 2 * tokens
    dma = pltpu.SemaphoreType.DMA
    anywhere = pl.BlockSpec(memory_space=pl.ANY)
    vmem = pl.BlockSpec(memory_space=pltpu.VMEM)
    gy, select, count = pl.pallas_call(
        functools.partial(prepare, (tokens, width)),
        out_shape=(
            jax.ShapeDtypeStruct((both, width), BF16),
            jax.ShapeDtypeStruct((both, both), BF16),
            jax.ShapeDtypeStruct((8, 128), F32),
        ),
        in_specs=[anywhere, vmem],
        out_specs=(vmem,) * 3,
        scratch_shapes=[
            pltpu.VMEM((2, tokens, width), BF16),
            pltpu.VMEM((2, 8, tokens), F32),
            dma(()), dma((2,)), dma((2,)),
        ],
        compiler_params=pltpu.CompilerParams(
            collective_id=0, has_side_effects=True, vmem_limit_bytes=62 * 2**20
        ),
        name="prepare",
    )(forget_cotangent, forget_labels)

    def stream(slots, collective_id):
        line = (nch, 2 * slots + both, CHUNK)
        macs = 3 * (slots + both) * width * (neurons // 2)
        return pl.pallas_call(
            functools.partial(kernel, (cols, rows, tokens, nch, slots)),
            out_shape=(
                jax.ShapeDtypeStruct((2, pad, CHUNK), F32),
                jax.ShapeDtypeStruct((tokens // rows, width), BF16),
            ),
            in_specs=[anywhere] * 4 + [vmem] * 6,
            out_specs=(vmem, vmem),
            scratch_shapes=[
                pltpu.VMEM((2, 2, tokens, width), BF16),
                pltpu.VMEM((2 * both, width), BF16),
                pltpu.VMEM((width, both), BF16),
                pltpu.VMEM((cols, 4, 8, tokens), F32),
                pltpu.VMEM((nch, width, CHUNK), BF16),
                pltpu.VMEM((nch, CHUNK, width), BF16),
                pltpu.VMEM(line, F32),
                pltpu.VMEM(line, BF16),
                pltpu.VMEM(line, BF16),
                pltpu.VMEM(line, BF16),
                pltpu.VMEM(line, BF16),
                pltpu.VMEM((both, width), F32),
                pltpu.VMEM((tokens, width), F32),
                pltpu.VMEM((rows - 1, tokens // rows, width), BF16),
                pltpu.VMEM((tokens, width), BF16),
                pltpu.VMEM((pad, CHUNK), F32),
                pltpu.VMEM((cols, pad, CHUNK), F32),
                pltpu.VMEM((2, pad, CHUNK), F32),
                dma((2,)), dma((2,)), dma((2,)), dma((cols - 1,)), dma((cols - 1,)),
                dma((nch,)), dma((nch,)),
                dma((2, nch)), dma((2, nch)), dma((2, nch)), dma((2, nch)),
                dma(()), dma(()),
                dma((rows - 1,)), dma((rows - 1,)),
                dma((cols - 1,)), dma((cols - 1,)),
                dma(()), dma(()),
            ],
            compiler_params=pltpu.CompilerParams(
                collective_id=collective_id, has_side_effects=True, vmem_limit_bytes=62 * 2**20
            ),
            cost_estimate=pl.CostEstimate(
                flops=2 * macs, bytes_accessed=2 * width * neurons, transcendentals=0
            ),
            name="stream_%d" % slots,
        )

    rest = (
        forget_tokens, retain_tokens, w_in, w_out, gy, select, ln_gain, b_in, pruned, b_out,
    )
    few = [slots * both // 256 for slots in SLOTS]
    index = sum((count[0, 0] > slots).astype(jnp.int32) for slots in few)
    branches = [
        lambda *args, slots=slots, i=i: tuple(stream(slots, 1 + i)(*args))
        for i, slots in enumerate(few + [both])
    ]
    saliency, retain_out = lax.switch(index, branches, *rest)
    return (saliency[:, :nch].reshape(neurons), retain_out)


def solution(mesh):
    in_specs = (
        P("dp", "col"),
        P("dp", "col"),
        P("dp"),
        P("dp", "col"),
        P("col"),
        P("col", "row"),
        P("row"),
        P("row", "col"),
        P("col"),
        P("row"),
    )
    out_specs = (P("row"), P(("dp", "row"), "col"))
    body = functools.partial(local, mesh.shape["col"], mesh.shape["row"])
    return jax.shard_map(body, mesh=mesh, in_specs=in_specs, out_specs=out_specs, check_vma=False)
```
